256 devices in a mesh: fsdp: 32 (over x, z), mp: 8 (over y, core).
Axes of the slice: x: 4, y: 4, z: 8, core: 2. Of those that a mesh axis runs over, the one named last changes fastest.
Arguments:
- grad: float32 [256, 512, 512], P('mp', 'fsdp')
- block_slot: int32 [256], P('mp'), may hold values from 0 to 63, as said below
- left_stat: float32 [64, 8, 512, 512], P('fsdp', 'mp')
- right_stat: float32 [64, 8, 512, 512], P('fsdp', 'mp')
- left_root: bfloat16 [64, 8, 512, 512], P('fsdp', 'mp')
- right_root: bfloat16 [64, 8, 512, 512], P('fsdp', 'mp')
Outputs:
- update: float32 [256, 512, 512], P('mp', 'fsdp')
- new_left: float32 [64, 8, 512, 512], P('fsdp', 'mp')
- new_right: float32 [64, 8, 512, 512], P('fsdp', 'mp')
The draws below stay inside these ranges and needn't reach their ends.
Inputs may be any that keep to these rules, and one draw needn't show every extreme that they name: `block_slot`: within each tensor-parallel group no slot is named twice; slot s belongs to fsdp owner s // 2, so an owner gets at most 2 blocks, and in every group some owner gets exactly 2.
All inputs are finite; a program needn't handle non-finite values.
Results may differ from the reference program's by a relative error of at most 0.017.
Values sent between devices are 32-bit elements; how exact they have to be, the bound alone decides.
A program may use at most 64 MiB of HBM per device.

```python
import math
import jax
import jax.numpy as jnp
from jax import lax

B = 512
CAP = 2
GROUPS = 8
GROUP_BLOCKS = 32
BLOCKS = 256
SLOTS = 64


def log_spread(base_key, shape, lowest, upper):
    return jnp.exp(jax.random.uniform(base_key, shape, jnp.float32, math.log(lowest), math.log(upper)))


def mixed_noise(base_key, shape):
    subkeys = jax.random.split(base_key, 1)
    normal_part = jax.random.normal(subkeys[0], shape, jnp.float32)
    return normal_part


def symmetric_factor(base_key, lowest, upper, off_scale):
    subkeys = jax.random.split(base_key, 2)
    leading = (SLOTS, GROUPS)
    diagonal = log_spread(subkeys[0], leading + (B,), lowest, upper)
    raw_noise = mixed_noise(subkeys[1], leading + (B, B))
    off_diagonal = (raw_noise + jnp.swapaxes(raw_noise, -1, -2)) * (off_scale / math.sqrt(2.0 * B))
    row_index = lax.broadcasted_iota(jnp.int32, (B, B), 0)
    col_index = lax.broadcasted_iota(jnp.int32, (B, B), 1)
    on_diagonal = row_index == col_index
    return jnp.where(on_diagonal, diagonal[..., :, None], off_diagonal)


def group_table(base_key):
    subkeys = jax.random.split(base_key, 2)
    shuffled = jax.random.permutation(subkeys[0], SLOTS).astype(jnp.int32)
    owner_full = shuffled[0] // CAP
    in_full = shuffled // CAP == owner_full
    needed = (shuffled == 0) | (shuffled == SLOTS - 1)
    priority = jnp.where(in_full, 2, jnp.where(needed, 0, 1)).astype(jnp.int32)
    order = jnp.argsort(priority, stable=True)
    remaining = shuffled[order][:SLOTS - CAP]
    full_owner = owner_full * CAP + jnp.arange(CAP, dtype=jnp.int32)
    sequence = jnp.concatenate([full_owner, remaining])[:GROUP_BLOCKS]
    mixing = jax.random.permutation(subkeys[1], GROUP_BLOCKS)
    return sequence[mixing].astype(jnp.int32)


def draw_block_slot(key, part):
    key = jax.random.fold_in(key, 3)
    tables = jax.vmap(lambda index: group_table(jax.random.fold_in(key, index)))(jnp.arange(GROUPS))
    return tables.reshape(BLOCKS).astype(jnp.int32)


def draw_grad(key, part):
    key = jax.random.fold_in(key, 5)
    subkeys = jax.random.split(key, 4)
    shape = (BLOCKS, B, B)
    noise = jax.random.normal(subkeys[0], shape, jnp.float32)
    row_top = 10.0
    block_scale = log_spread(subkeys[1], (BLOCKS, 1, 1), 0.5, 5.0)
    row_scale = log_spread(subkeys[2], (BLOCKS, B, 1), 1.0, row_top)
    col_scale = log_spread(subkeys[3], (BLOCKS, 1, B), 1.0, 10.0)
    return noise * block_scale * row_scale * col_scale / (3.0 * math.sqrt(B))


def draw_left_stat(key, part):
    key = jax.random.fold_in(key, 11)
    return symmetric_factor(key, 1.0, 10.0, 2.0)


def draw_right_stat(key, part):
    key = jax.random.fold_in(key, 13)
    return symmetric_factor(key, 1.0, 10.0, 2.0)


def draw_left_root(key, part):
    key = jax.random.fold_in(key, 17)
    return symmetric_factor(key, 0.3, 3.0, 0.6).astype(jnp.bfloat16)


def draw_right_root(key, part):
    key = jax.random.fold_in(key, 19)
    return symmetric_factor(key, 0.3, 3.0, 0.6).astype(jnp.bfloat16)


def setup_inputs(seed: int = 0) -> dict:
    key_list = jax.random.split(jax.random.key(seed), 7)
    return {
        "grad": draw_grad(jax.random.fold_in(key_list[6], 71), 0),
        "block_slot": draw_block_slot(jax.random.fold_in(key_list[6], 71), 0),
        "left_stat": draw_left_stat(jax.random.fold_in(key_list[6], 71), 0),
        "right_stat": draw_right_stat(jax.random.fold_in(key_list[6], 71), 0),
        "left_root": draw_left_root(jax.random.fold_in(key_list[6], 71), 0),
        "right_root": draw_right_root(jax.random.fold_in(key_list[6], 71), 0),
    }


decay_rate = 0.9
epsilon = 1e-06
exact_mode = lax.Precision.HIGHEST

def reference(grad, block_slot, left_stat, right_stat, left_root, right_root):
    group_of = (jnp.arange(BLOCKS) // GROUP_BLOCKS).astype(jnp.int32)

    def per_block(packed):
        block_grad, slot_index, group_index = packed
        left_factor = left_root[slot_index, group_index].astype(jnp.float32)
        right_factor = right_root[slot_index, group_index].astype(jnp.float32)
        left_prod = jnp.dot(block_grad, block_grad.T, precision=exact_mode, preferred_element_type=jnp.float32)
        right_prod = jnp.dot(block_grad.T, block_grad, precision=exact_mode, preferred_element_type=jnp.float32)
        precond = jnp.dot(left_factor, block_grad, precision=exact_mode, preferred_element_type=jnp.float32)
        precond = jnp.dot(precond, right_factor, precision=exact_mode, preferred_element_type=jnp.float32)
        grad_sq = jnp.sum(block_grad * block_grad)
        pre_sq = jnp.sum(precond * precond)
        direction = precond * (jnp.sqrt(grad_sq) / (jnp.sqrt(pre_sq) + epsilon))
        return (left_prod, right_prod, direction)
    left_prods, right_prods, directions = lax.map(per_block, (grad, block_slot, group_of))
    left_sum = jnp.zeros_like(left_stat).at[block_slot, group_of].add(left_prods)
    right_sum = jnp.zeros_like(right_stat).at[block_slot, group_of].add(right_prods)
    new_left = decay_rate * left_stat + (1.0 - decay_rate) * left_sum
    new_right = decay_rate * right_stat + (1.0 - decay_rate) * right_sum
    total_sq = jnp.sum(directions * directions)
    root_mean = jnp.sqrt(total_sq / float(BLOCKS * B * B) + epsilon)
    update = directions / root_mean
    return (update, new_left, new_right)
```

```python
import functools

import jax
import jax.numpy as jnp
from jax import lax
from jax.experimental import pallas as pl
from jax.experimental.pallas import tpu as pltpu
from jax.sharding import PartitionSpec as P

decay_rate = 0.9
epsilon = 1e-06
MESH = pl.DeviceIdType.MESH
F32 = jnp.float32
BF16 = jnp.bfloat16


def split(x):
    high = x.astype(BF16)
    return high, (x - high.astype(F32)).astype(BF16)


def dot(a, b, a_dim=1, b_dim=0):
    return lax.dot_general(a, b, (((a_dim,), (b_dim,)), ((), ())), preferred_element_type=F32)


def kernel(
    cfg,
    source_ref,
    slot_ref,
    grad_hbm,
    ls_hbm,
    rs_hbm,
    lr_hbm,
    rr_hbm,
    update_ref,
    nl_hbm,
    nr_hbm,
    grad,
    stage,
    blocks,
    dirs,
    back,
    ls,
    rs,
    lr,
    rr,
    high,
    low,
    sq_out,
    sq_group,
    sq_sum,
    sq_all,
    in_sem,
    out_sem,
    fsend,
    frecv,
    rsend,
    rrecv,
    qsend,
    qrecv,
):
    fs, mps, cap, rows, width, inner, entries = cfg
    outer = fs // inner
    me = lax.axis_index("fsdp")
    lane = lax.axis_index("mp")
    me_out, me_in = me // inner, me % inner
    tile = 128
    tiles = width // tile

    def peer(d):
        d_out, d_in = d // inner, d % inner
        return ((me_out + d_out) % outer) * inner + (me_in + d_in) % inner

    def rows_of(device):
        return pl.ds(pl.multiple_of(device * rows, rows), rows)

    barrier = pltpu.get_barrier_semaphore()

    def greet(d, c):
        pl.semaphore_signal(barrier, inc=1, device_id=(peer(d), lane), device_id_type=MESH)
        return c

    lax.fori_loop(1, fs, greet, 0)

    def greet_lane(d, c):
        pl.semaphore_signal(barrier, inc=1, device_id=(me, (lane + d) % mps), device_id_type=MESH)
        return c

    lax.fori_loop(1, mps, greet_lane, 0)

    loads = [
        pltpu.make_async_copy(a, b, in_sem.at[i])
        for i, (a, b) in enumerate(
            ((grad_hbm, grad), (lr_hbm, lr), (rr_hbm, rr), (ls_hbm, ls), (rs_hbm, rs))
        )
    ]
    for load in loads:
        load.start()
    loads[0].wait()

    for a in range(cap):

        def fill(o, c, a=a):
            named = source_ref[o * cap + a]
            chunk = grad[jnp.maximum(named - 1, 0)]
            stage[a, o] = jnp.where(named > 0, chunk, 0.0)
            return c

        lax.fori_loop(0, fs, fill, 0)

    pl.semaphore_wait(barrier, fs - 1 + mps - 1)

    for a in range(cap):

        def send(d, c, a=a):
            p = peer(d)
            pltpu.make_async_remote_copy(
                src_ref=stage.at[a, p],
                dst_ref=blocks.at[a, rows_of(me)],
                send_sem=fsend.at[a],
                recv_sem=frecv.at[a],
                device_id=(p, lane),
                device_id_type=MESH,
            ).start()
            return c

        lax.fori_loop(1, fs, send, 0)
        blocks[a, rows_of(me)] = stage[a, me]

    for load in loads[1:]:
        load.wait()

    def give_back(a):
        def send(d, c):
            p = peer(d)
            pltpu.make_async_remote_copy(
                src_ref=dirs.at[a, rows_of(p)],
                dst_ref=back.at[a, me],
                send_sem=rsend.at[a],
                recv_sem=rrecv.at[a],
                device_id=(p, lane),
                device_id_type=MESH,
            ).start()
            return c

        lax.fori_loop(1, fs, send, 0)
        back[a, me] = dirs[a, rows_of(me)]

    def part(t):
        return pl.ds(pl.multiple_of(t * tile, tile), tile)

    def total(x):
        return jnp.sum(x, axis=(0, 1), keepdims=True)

    def precondition(a):
        def cut(t, sq):
            g = blocks[a, part(t)]
            h, l = split(g)
            high[a, part(t)] = h
            low[a, part(t)] = l
            return sq + total(g * g)

        grad_sq = lax.fori_loop(0, tiles, cut, jnp.zeros((1, 1), F32))

        def multiply(t, sq):
            root = lr[a, part(t)]
            h, l = split(dot(root, high[a]) + dot(root, low[a]))
            p = dot(h, rr[a]) + dot(l, rr[a])
            dirs[a, part(t)] = p
            return sq + total(p * p)

        pre_sq = lax.fori_loop(0, tiles, multiply, jnp.zeros((1, 1), F32))
        ratio = jnp.sqrt(grad_sq) / (jnp.sqrt(pre_sq) + epsilon)

        def graft(t, sq):
            p = dirs[a, part(t)] * ratio
            dirs[a, part(t)] = p
            return sq + total(p * p)

        return lax.fori_loop(0, tiles, graft, jnp.zeros((1, 1), F32))

    def statistics(a):
        def left(t, c):
            h, l = high[a, part(t)], low[a, part(t)]
            prod = dot(h, high[a], 1, 1) + dot(h, low[a], 1, 1) + dot(l, high[a], 1, 1)
            ls[a, part(t)] = decay_rate * ls[a, part(t)] + (1.0 - decay_rate) * prod
            return c

        lax.fori_loop(0, tiles, left, 0)
        for t in range(tiles):
            cols = pl.ds(t * tile, tile)
            h, l = high[a, :, cols], low[a, :, cols]
            prod = dot(h, high[a], 0, 0) + dot(h, low[a], 0, 0) + dot(l, high[a], 0, 0)
            rs[a, cols] = decay_rate * rs[a, cols] + (1.0 - decay_rate) * prod

    def wait_for(ref, sem):
        pltpu.make_async_copy(ref, ref, sem).wait()

    others = fs - 1
    squares = jnp.zeros((1, 1), F32)
    for a in range(cap):
        wait_for(blocks.at[a, pl.ds(0, others * rows)], frecv.at[a])
        squares = squares + precondition(a)
        give_back(a)
        if a < cap - 1:
            statistics(a)

    sq_out[...] = jnp.broadcast_to(squares, sq_out.shape)

    def send_square(d, c):
        pltpu.make_async_remote_copy(
            src_ref=sq_out,
            dst_ref=sq_group.at[me],
            send_sem=qsend.at[0],
            recv_sem=qrecv.at[0],
            device_id=(peer(d), lane),
            device_id_type=MESH,
        ).start()
        return c

    lax.fori_loop(1, fs, send_square, 0)
    sq_group[me] = sq_out[...]
    statistics(cap - 1)
    stores = [
        pltpu.make_async_copy(a, b, out_sem.at[i])
        for i, (a, b) in enumerate(((ls, nl_hbm), (rs, nr_hbm)))
    ]
    for store in stores:
        store.start()
    wait_for(sq_group.at[pl.ds(0, others)], qrecv.at[0])
    sq_sum[...] = jnp.sum(sq_group[...], axis=0)

    def send_sum(d, c):
        pltpu.make_async_remote_copy(
            src_ref=sq_sum,
            dst_ref=sq_all.at[lane],
            send_sem=qsend.at[1],
            recv_sem=qrecv.at[1],
            device_id=(me, (lane + d) % mps),
            device_id_type=MESH,
        ).start()
        return c

    lax.fori_loop(1, mps, send_sum, 0)
    sq_all[lane] = sq_sum[...]
    wait_for(sq_all.at[pl.ds(0, mps - 1)], qrecv.at[1])
    total_sq = jnp.sum(sq_all[...], axis=0)[0:1, 0:1]
    scale = 1.0 / jnp.sqrt(total_sq / entries + epsilon)

    for a in range(cap):
        wait_for(back.at[a, pl.ds(0, others)], rrecv.at[a])

    def place(j, c):
        s = slot_ref[j]
        update_ref[j] = back[s % cap, s // cap] * scale
        return c

    lax.fori_loop(0, update_ref.shape[0], place, 0)

    for a in range(cap):
        wait_for(stage.at[a, pl.ds(0, others)], fsend.at[a])
        wait_for(dirs.at[a, pl.ds(0, others * rows)], rsend.at[a])
    wait_for(sq_group.at[pl.ds(0, others)], qsend.at[0])
    wait_for(sq_all.at[pl.ds(0, mps - 1)], qsend.at[1])
    for store in stores:
        store.wait()


def local(inner, grad, block_slot, left_stat, right_stat, left_root, right_root):
    fs, mps = lax.axis_size("fsdp"), lax.axis_size("mp")
    cap = left_stat.shape[0]
    count, rows, width = grad.shape
    slots = jnp.arange(fs * cap, dtype=jnp.int32)
    matches = block_slot[None, :] == slots[:, None]
    source = jnp.sum(
        jnp.where(matches, jnp.arange(1, count + 1, dtype=jnp.int32)[None, :], 0), axis=1
    )
    entries = float(count * mps * width * width)
    square = (cap, width, width)
    smem = pl.BlockSpec(memory_space=pltpu.SMEM)
    anywhere = pl.BlockSpec(memory_space=pl.ANY)
    vmem = pl.BlockSpec(memory_space=pltpu.VMEM)
    update, new_left, new_right = pl.pallas_call(
        functools.partial(kernel, (fs, mps, cap, rows, width, inner, entries)),
        out_shape=(
            jax.ShapeDtypeStruct(grad.shape, F32),
            jax.ShapeDtypeStruct(square, F32),
            jax.ShapeDtypeStruct(square, F32),
        ),
        in_specs=[smem, smem] + [anywhere] * 5,
        out_specs=(vmem, anywhere, anywhere),
        scratch_shapes=[
            pltpu.VMEM(grad.shape, F32),
            pltpu.VMEM((cap, fs, rows, width), F32),
            pltpu.VMEM(square, F32),
            pltpu.VMEM(square, F32),
            pltpu.VMEM((cap, fs, rows, width), F32),
            pltpu.VMEM(square, F32),
            pltpu.VMEM(square, F32),
            pltpu.VMEM(square, BF16),
            pltpu.VMEM(square, BF16),
            pltpu.VMEM(square, BF16),
            pltpu.VMEM(square, BF16),
            pltpu.VMEM((8, 128), F32),
            pltpu.VMEM((fs, 8, 128), F32),
            pltpu.VMEM((8, 128), F32),
            pltpu.VMEM((mps, 8, 128), F32),
            pltpu.SemaphoreType.DMA((5,)),
            pltpu.SemaphoreType.DMA((2,)),
            pltpu.SemaphoreType.DMA((cap,)),
            pltpu.SemaphoreType.DMA((cap,)),
            pltpu.SemaphoreType.DMA((cap,)),
            pltpu.SemaphoreType.DMA((cap,)),
            pltpu.SemaphoreType.DMA((2,)),
            pltpu.SemaphoreType.DMA((2,)),
        ],
        compiler_params=pltpu.CompilerParams(
            collective_id=0, has_side_effects=True, vmem_limit_bytes=48 << 20
        ),
        cost_estimate=pl.CostEstimate(
            flops=20 * cap * width**3, bytes_accessed=12 << 20, transcendentals=0
        ),
    )(
        source,
        block_slot,
        grad,
        left_stat[:, 0],
        right_stat[:, 0],
        left_root[:, 0],
        right_root[:, 0],
    )
    return (update, new_left[:, None], new_right[:, None])


def solution(mesh):
    fs = mesh.shape["fsdp"]
    inner = 8 if fs % 8 == 0 else fs
    placed = (
        P("mp", "fsdp", None),
        P("mp"),
        P("fsdp", "mp", None, None),
        P("fsdp", "mp", None, None),
        P("fsdp", "mp", None, None),
        P("fsdp", "mp", None, None),
    )
    return jax.shard_map(
        functools.partial(local, inner),
        mesh=mesh,
        in_specs=placed,
        out_specs=(P("mp", "fsdp", None), P("fsdp", "mp", None, None), P("fsdp", "mp", None, None)),
        check_vma=False,
    )
```

```python
import functools

import jax
import jax.numpy as jnp
from jax import lax
from jax.experimental import pallas as pl
from jax.experimental.pallas import tpu as pltpu
from jax.sharding import PartitionSpec as P

decay_rate = 0.9
epsilon = 1e-06
MESH = pl.DeviceIdType.MESH
F32 = jnp.float32
BF16 = jnp.bfloat16


def split(x):
    high = x.astype(BF16)
    return high, (x - high.astype(F32)).astype(BF16)


def dot(a, b, a_dim=1, b_dim=0):
    return lax.dot_general(a, b, (((a_dim,), (b_dim,)), ((), ())), preferred_element_type=F32)


def kernel(
    cfg,
    slot_hbm,
    grad_hbm,
    ls_hbm,
    rs_hbm,
    lr_hbm,
    rr_hbm,
    update,
    ls,
    rs,
    back,
    slot,
    table,
    source,
    grad,
    stage,
    blocks,
    dirs,
    lr,
    rr,
    high,
    low,
    sq_out,
    sq_group,
    sq_sum,
    sq_all,
    in_sem,
    fsend,
    frecv,
    rsend,
    rrecv,
    qsend,
    qrecv,
):
    fs, mps, cap, rows, width, inner, entries = cfg
    outer = fs // inner
    me = lax.axis_index("fsdp")
    lane = lax.axis_index("mp")
    me_out, me_in = me // inner, me % inner
    tile = 128
    tiles = width // tile

    turn = 1 - 2 * (me_in % 2)

    def zigzag(k, size):
        return (k % 2) * ((k + 1) // 2) + (1 - k % 2) * (size - k // 2)

    def peer(d):
        d_out, d_in = zigzag(d // inner, outer), zigzag(d % inner, inner)
        p_out = (me_out + turn * d_out + outer) % outer
        return p_out * inner + (me_in + turn * d_in + inner) % inner

    def rows_of(device):
        return pl.ds(pl.multiple_of(device * rows, rows), rows)

    pairs = (
        (slot_hbm, slot),
        (grad_hbm, grad),
        (lr_hbm, lr),
        (rr_hbm, rr),
        (ls_hbm, ls),
        (rs_hbm, rs),
    )
    loads = [pltpu.make_async_copy(a, b, in_sem.at[i]) for i, (a, b) in enumerate(pairs)]
    loads[0].start()
    loads[1].start()

    barrier = pltpu.get_barrier_semaphore()

    def greet(d, c):
        pl.semaphore_signal(barrier, inc=1, device_id=(peer(d), lane), device_id_type=MESH)
        return c

    lax.fori_loop(1, fs, greet, 0)

    def greet_lane(d, c):
        pl.semaphore_signal(barrier, inc=1, device_id=(me, (lane + d) % mps), device_id_type=MESH)
        return c

    lax.fori_loop(1, mps, greet_lane, 0)

    loads[0].wait()
    ids = lax.broadcasted_iota(jnp.int32, table.shape, 1)

    def name(j, named):
        return jnp.where(ids == slot[j], j + 1, named)

    table[...] = lax.fori_loop(0, grad.shape[0], name, jnp.zeros(table.shape, jnp.int32))
    move = pltpu.make_async_copy(table, source, in_sem.at[len(pairs)])
    move.start()
    move.wait()
    loads[1].wait()

    for a in range(cap):

        def fill(o, c, a=a):
            named = source[0, o * cap + a]
            chunk = grad[jnp.maximum(named - 1, 0)]
            stage[a, o] = jnp.where(named > 0, chunk, 0.0)
            return c

        lax.fori_loop(0, fs, fill, 0)
        if a == 0:
            pl.semaphore_wait(barrier, fs - 1 + mps - 1)

        def send(d, c, a=a):
            p = peer(d)
            pltpu.make_async_remote_copy(
                src_ref=stage.at[a, p],
                dst_ref=blocks.at[a, rows_of(me)],
                send_sem=fsend.at[a],
                recv_sem=frecv.at[a],
                device_id=(p, lane),
                device_id_type=MESH,
            ).start()
            return c

        lax.fori_loop(1, fs, send, 0)
        blocks[a, rows_of(me)] = stage[a, me]

    for load in loads[2:]:
        load.start()
    for load in loads[2:]:
        load.wait()

    def give_back(a, first, last):
        def send(d, c):
            p = peer(d)
            pltpu.make_async_remote_copy(
                src_ref=dirs.at[a, rows_of(p)],
                dst_ref=back.at[a, me],
                send_sem=rsend.at[a],
                recv_sem=rrecv.at[a],
                device_id=(p, lane),
                device_id_type=MESH,
            ).start()
            return c

        lax.fori_loop(first, last, send, 0)

    def part(t):
        return pl.ds(pl.multiple_of(t * tile, tile), tile)

    def total(x):
        return jnp.sum(x, axis=(0, 1), keepdims=True)

    def precondition(a):
        def cut(t, sq):
            g = blocks[a, part(t)]
            h, l = split(g)
            high[a, part(t)] = h
            low[a, part(t)] = l
            return sq + total(g * g)

        grad_sq = lax.fori_loop(0, tiles, cut, jnp.zeros((1, 1), F32))

        def multiply(t, sq):
            root = lr[a, part(t)]
            h, l = split(dot(root, high[a]) + dot(root, low[a]))
            p = dot(h, rr[a]) + dot(l, rr[a])
            dirs[a, part(t)] = p
            return sq + total(p * p)

        pre_sq = lax.fori_loop(0, tiles, multiply, jnp.zeros((1, 1), F32))
        ratio = jnp.sqrt(grad_sq) / (jnp.sqrt(pre_sq) + epsilon)

        def graft(t, sq):
            p = dirs[a, part(t)] * ratio
            dirs[a, part(t)] = p
            return sq + total(p * p)

        return lax.fori_loop(0, tiles, graft, jnp.zeros((1, 1), F32))

    def statistics(a):
        def left(t, c):
            h, l = high[a, part(t)], low[a, part(t)]
            prod = dot(h, high[a], 1, 1) + dot(h, low[a], 1, 1) + dot(l, high[a], 1, 1)
            ls[a, part(t)] = decay_rate * ls[a, part(t)] + (1.0 - decay_rate) * prod
            return c

        lax.fori_loop(0, tiles, left, 0)
        for t in range(tiles):
            cols = pl.ds(t * tile, tile)
            h, l = high[a, :, cols], low[a, :, cols]
            prod = dot(h, high[a], 0, 0) + dot(h, low[a], 0, 0) + dot(l, high[a], 0, 0)
            rs[a, cols] = decay_rate * rs[a, cols] + (1.0 - decay_rate) * prod

    def wait_for(ref, sem):
        pltpu.make_async_copy(ref, ref, sem).wait()

    others = fs - 1

    def send_square(d, c):
        pltpu.make_async_remote_copy(
            src_ref=sq_out,
            dst_ref=sq_group.at[me],
            send_sem=qsend.at[0],
            recv_sem=qrecv.at[0],
            device_id=(peer(d), lane),
            device_id_type=MESH,
        ).start()
        return c

    def send_sum(d, c):
        pltpu.make_async_remote_copy(
            src_ref=sq_sum,
            dst_ref=sq_all.at[lane],
            send_sem=qsend.at[1],
            recv_sem=qrecv.at[1],
            device_id=(me, (lane + d) % mps),
            device_id_type=MESH,
        ).start()
        return c

    squares = jnp.zeros((1, 1), F32)
    for a in range(cap):
        wait_for(blocks.at[a, pl.ds(0, others * rows)], frecv.at[a])
        squares = squares + precondition(a)
        if a < cap - 1:
            give_back(a, 1, fs)
            statistics(a)
        else:
            sq_out[...] = jnp.broadcast_to(squares, sq_out.shape)
            lax.fori_loop(1, fs, send_square, 0)
            sq_group[me] = sq_out[...]
            give_back(a, 1, fs // 2)
            wait_for(sq_group.at[pl.ds(0, others)], qrecv.at[0])
            sq_sum[...] = jnp.sum(sq_group[...], axis=0)
            lax.fori_loop(1, mps, send_sum, 0)
            sq_all[lane] = sq_sum[...]
            give_back(a, fs // 2, fs)
            statistics(a)
        back[a, me] = dirs[a, rows_of(me)]

    wait_for(sq_all.at[pl.ds(0, mps - 1)], qrecv.at[1])
    total_sq = jnp.sum(sq_all[...], axis=0)
    scale = (1.0 / jnp.sqrt(total_sq / entries + epsilon))[0:1, 0:1]

    for a in range(cap):
        wait_for(stage.at[a, pl.ds(0, others)], fsend.at[a])
        wait_for(dirs.at[a, pl.ds(0, others * rows)], rsend.at[a])
    wait_for(sq_group.at[pl.ds(0, others)], qsend.at[0])
    wait_for(sq_all.at[pl.ds(0, mps - 1)], qsend.at[1])
    for a in range(cap):
        wait_for(back.at[a, pl.ds(0, others)], rrecv.at[a])

    def place(j, c):
        s = slot[j]
        update[j] = back[s % cap, s // cap] * scale
        return c

    lax.fori_loop(0, update.shape[0], place, 0, unroll=4)


def finish(update, ls, rs, update_hbm, nl_hbm, nr_hbm, sem):
    pairs = ((update, update_hbm), (ls, nl_hbm), (rs, nr_hbm))
    stores = [pltpu.make_async_copy(a, b, sem.at[i]) for i, (a, b) in enumerate(pairs)]
    for store in stores:
        store.start()
    for store in stores:
        store.wait()


def far(x):
    return pltpu.with_memory_space_constraint(x, pltpu.HBM)


def local(inner, grad, block_slot, left_stat, right_stat, left_root, right_root):
    fs, mps = lax.axis_size("fsdp"), lax.axis_size("mp")
    cap = left_stat.shape[0]
    count, rows, width = grad.shape
    entries = float(count * mps * width * width)
    square = (cap, width, width)
    chunks = (cap, fs, rows, width)
    table = (1, -(-fs * cap // 128) * 128)
    hbm = pl.BlockSpec(memory_space=pltpu.HBM)
    vmem = pl.BlockSpec(memory_space=pltpu.VMEM)
    update, left, right = pl.pallas_call(
        functools.partial(kernel, (fs, mps, cap, rows, width, inner, entries)),
        out_shape=(
            pltpu.VMEM(grad.shape, F32),
            pltpu.VMEM(square, F32),
            pltpu.VMEM(square, F32),
        ),
        in_specs=[hbm] * 6,
        out_specs=(vmem,) * 3,
        scratch_shapes=[
            pltpu.VMEM(chunks, F32),
            pltpu.SMEM(block_slot.shape, jnp.int32),
            pltpu.VMEM(table, jnp.int32),
            pltpu.SMEM(table, jnp.int32),
            pltpu.VMEM(grad.shape, F32),
            pltpu.VMEM(chunks, F32),
            pltpu.VMEM(square, F32),
            pltpu.VMEM(square, F32),
            pltpu.VMEM(square, BF16),
            pltpu.VMEM(square, BF16),
            pltpu.VMEM(square, BF16),
            pltpu.VMEM(square, BF16),
            pltpu.VMEM((1, 128), F32),
            pltpu.VMEM((fs, 1, 128), F32),
            pltpu.VMEM((1, 128), F32),
            pltpu.VMEM((mps, 1, 128), F32),
            pltpu.SemaphoreType.DMA((7,)),
            pltpu.SemaphoreType.DMA((cap,)),
            pltpu.SemaphoreType.DMA((cap,)),
            pltpu.SemaphoreType.DMA((cap,)),
            pltpu.SemaphoreType.DMA((cap,)),
            pltpu.SemaphoreType.DMA((2,)),
            pltpu.SemaphoreType.DMA((2,)),
        ],
        compiler_params=pltpu.CompilerParams(
            collective_id=0, has_side_effects=True, vmem_limit_bytes=40 << 20
        ),
        cost_estimate=pl.CostEstimate(
            flops=20 * cap * width**3, bytes_accessed=12 << 20, transcendentals=0
        ),
    )(
        far(block_slot),
        far(grad),
        far(left_stat[:, 0]),
        far(right_stat[:, 0]),
        far(left_root[:, 0]),
        far(right_root[:, 0]),
    )
    update, new_left, new_right = pl.pallas_call(
        finish,
        out_shape=(
            jax.ShapeDtypeStruct(grad.shape, F32),
            jax.ShapeDtypeStruct(square, F32),
            jax.ShapeDtypeStruct(square, F32),
        ),
        in_specs=[vmem] * 3,
        out_specs=(hbm,) * 3,
        scratch_shapes=[pltpu.SemaphoreType.DMA((3,))],
        compiler_params=pltpu.CompilerParams(vmem_limit_bytes=16 << 20),
        cost_estimate=pl.CostEstimate(flops=0, bytes_accessed=5 << 20, transcendentals=0),
    )(update, left, right)
    return (update, new_left[:, None], new_right[:, None])


def solution(mesh):
    fs = mesh.shape["fsdp"]
    inner = 8 if fs % 8 == 0 else fs
    placed = (
        P("mp", "fsdp", None),
        P("mp"),
        P("fsdp", "mp", None, None),
        P("fsdp", "mp", None, None),
        P("fsdp", "mp", None, None),
        P("fsdp", "mp", None, None),
    )
    return jax.shard_map(
        functools.partial(local, inner),
        mesh=mesh,
        in_specs=placed,
        out_specs=(P("mp", "fsdp", None), P("fsdp", "mp", None, None), P("fsdp", "mp", None, None)),
        check_vma=False,
    )
```

```python
import functools

import jax
import jax.numpy as jnp
from jax import lax
from jax.experimental import pallas as pl
from jax.experimental.pallas import tpu as pltpu
from jax.sharding import PartitionSpec as P

decay_rate = 0.9
epsilon = 1e-06
MESH = pl.DeviceIdType.MESH
F32 = jnp.float32
BF16 = jnp.bfloat16


def split(x):
    high = x.astype(BF16)
    return high, (x - high.astype(F32)).astype(BF16)


def dot(a, b, a_dim=1, b_dim=0):
    return lax.dot_general(a, b, (((a_dim,), (b_dim,)), ((), ())), preferred_element_type=F32)


def kernel(
    cfg,
    slot_hbm,
    grad_hbm,
    ls_hbm,
    rs_hbm,
    lr_hbm,
    rr_hbm,
    update,
    ls,
    rs,
    back,
    slot,
    table,
    source,
    grad,
    stage,
    blocks,
    dirs,
    lr,
    rr,
    high,
    low,
    sq_out,
    sq_group,
    sq_sum,
    sq_all,
    in_sem,
    fsend,
    frecv,
    rsend,
    rrecv,
    qsend,
    qrecv,
):
    fs, mps, cap, rows, width, inner, entries = cfg
    outer = fs // inner
    me = lax.axis_index("fsdp")
    lane = lax.axis_index("mp")
    me_out, me_in = me // inner, me % inner
    tile = 128
    tiles = width // tile

    turn = 1 - 2 * (me_in % 2)

    def zigzag(k, size):
        return (k + 1) // 2 if k % 2 else (size - k // 2) % size

    outs = [((me_out + turn * zigzag(k, outer) + outer) % outer) * inner for k in range(outer)]
    ins = [(me_in + turn * zigzag(k, inner) + inner) % inner for k in range(inner)]
    peers = [outs[d // inner] + ins[d % inner] for d in range(fs)]
    lanes = [(lane + d) % mps for d in range(mps)]

    def peer(d):
        k, j = d // inner, d % inner
        k = (k % 2) * ((k + 1) // 2) + (1 - k % 2) * (outer - k // 2)
        j = (j % 2) * ((j + 1) // 2) + (1 - j % 2) * (inner - j // 2)
        p_out = (me_out + turn * k + outer) % outer
        return p_out * inner + (me_in + turn * j + inner) % inner

    def rows_of(device):
        return pl.ds(pl.multiple_of(device * rows, rows), rows)

    pairs = (
        (slot_hbm, slot),
        (grad_hbm, grad),
        (lr_hbm, lr),
        (rr_hbm, rr),
        (ls_hbm, ls),
        (rs_hbm, rs),
    )
    loads = [pltpu.make_async_copy(a, b, in_sem.at[i]) for i, (a, b) in enumerate(pairs)]
    loads[0].start()
    loads[1].start()

    barrier = pltpu.get_barrier_semaphore()

    for f, l in [(p, lane) for p in peers[1:]] + [(me, l) for l in lanes[1:]]:
        pl.semaphore_signal(barrier, inc=1, device_id=(f, l), device_id_type=MESH)

    loads[0].wait()
    ids = lax.broadcasted_iota(jnp.int32, table.shape, 1)

    def name(j, named):
        return jnp.where(ids == slot[j], j + 1, named)

    table[...] = lax.fori_loop(0, grad.shape[0], name, jnp.zeros(table.shape, jnp.int32))
    move = pltpu.make_async_copy(table, source, in_sem.at[len(pairs)])
    move.start()
    move.wait()
    loads[1].wait()

    for a in range(cap):

        def fill(o, c, a=a):
            named = source[0, o * cap + a]
            chunk = grad[jnp.maximum(named - 1, 0)]
            stage[a, o] = jnp.where(named > 0, chunk, 0.0)
            return c

        lax.fori_loop(0, fs, fill, 0)
        if a == 0:
            pl.semaphore_wait(barrier, fs - 1 + mps - 1)

        def send(d, c, a=a):
            p = peer(d)
            pltpu.make_async_remote_copy(
                src_ref=stage.at[a, p],
                dst_ref=blocks.at[a, rows_of(me)],
                send_sem=fsend.at[a],
                recv_sem=frecv.at[a],
                device_id=(p, lane),
                device_id_type=MESH,
            ).start()
            return c

        lax.fori_loop(1, fs, send, 0)
        blocks[a, rows_of(me)] = stage[a, me]

    for load in loads[2:]:
        load.start()
    for load in loads[2:]:
        load.wait()

    def give_back(a, first, last):
        def send(d, c):
            p = peer(d)
            pltpu.make_async_remote_copy(
                src_ref=dirs.at[a, rows_of(p)],
                dst_ref=back.at[a, me],
                send_sem=rsend.at[a],
                recv_sem=rrecv.at[a],
                device_id=(p, lane),
                device_id_type=MESH,
            ).start()
            return c

        lax.fori_loop(first, last, send, 0)

    def part(t):
        return pl.ds(pl.multiple_of(t * tile, tile), tile)

    def total(x):
        return jnp.sum(x, axis=(0, 1), keepdims=True)

    def precondition(a):
        def cut(t, sq):
            g = blocks[a, part(t)]
            h, l = split(g)
            high[a, part(t)] = h
            low[a, part(t)] = l
            return sq + total(g * g)

        grad_sq = lax.fori_loop(0, tiles, cut, jnp.zeros((1, 1), F32))

        def multiply(t, sq):
            root = lr[a, part(t)]
            h, l = split(dot(root, high[a]) + dot(root, low[a]))
            p = dot(h, rr[a]) + dot(l, rr[a])
            dirs[a, part(t)] = p
            return sq + total(p * p)

        pre_sq = lax.fori_loop(0, tiles, multiply, jnp.zeros((1, 1), F32))
        ratio = jnp.sqrt(grad_sq) / (jnp.sqrt(pre_sq) + epsilon)

        def graft(t, sq):
            p = dirs[a, part(t)] * ratio
            dirs[a, part(t)] = p
            return sq + total(p * p)

        return lax.fori_loop(0, tiles, graft, jnp.zeros((1, 1), F32))

    def statistics(a):
        def left(t, c):
            h, l = high[a, part(t)], low[a, part(t)]
            prod = dot(h, high[a], 1, 1) + dot(h, low[a], 1, 1) + dot(l, high[a], 1, 1)
            ls[a, part(t)] = decay_rate * ls[a, part(t)] + (1.0 - decay_rate) * prod
            return c

        lax.fori_loop(0, tiles, left, 0)
        for t in range(tiles):
            cols = pl.ds(t * tile, tile)
            h, l = high[a, :, cols], low[a, :, cols]
            prod = dot(h, high[a], 0, 0) + dot(h, low[a], 0, 0) + dot(l, high[a], 0, 0)
            rs[a, cols] = decay_rate * rs[a, cols] + (1.0 - decay_rate) * prod

    def wait_for(ref, sem):
        pltpu.make_async_copy(ref, ref, sem).wait()

    others = fs - 1

    def send_square(d, c):
        pltpu.make_async_remote_copy(
            src_ref=sq_out,
            dst_ref=sq_group.at[me],
            send_sem=qsend.at[0],
            recv_sem=qrecv.at[0],
            device_id=(peer(d), lane),
            device_id_type=MESH,
        ).start()
        return c

    def send_sum(d, c):
        pltpu.make_async_remote_copy(
            src_ref=sq_sum,
            dst_ref=sq_all.at[lane],
            send_sem=qsend.at[1],
            recv_sem=qrecv.at[1],
            device_id=(me, (lane + d) % mps),
            device_id_type=MESH,
        ).start()
        return c

    squares = jnp.zeros((1, 1), F32)
    for a in range(cap):
        wait_for(blocks.at[a, pl.ds(0, others * rows)], frecv.at[a])
        squares = squares + precondition(a)
        if a < cap - 1:
            give_back(a, 1, fs)
            statistics(a)
        else:
            sq_out[...] = jnp.broadcast_to(squares, sq_out.shape)
            lax.fori_loop(1, fs, send_square, 0)
            sq_group[me] = sq_out[...]
            give_back(a, 1, fs // 2)
            wait_for(sq_group.at[pl.ds(0, others)], qrecv.at[0])
            sq_sum[...] = jnp.sum(sq_group[...], axis=0)
            lax.fori_loop(1, mps, send_sum, 0)
            sq_all[lane] = sq_sum[...]
            give_back(a, fs // 2, fs)
            statistics(a)
        back[a, me] = dirs[a, rows_of(me)]

    wait_for(sq_all.at[pl.ds(0, mps - 1)], qrecv.at[1])
    total_sq = jnp.sum(sq_all[...], axis=0)
    scale = (1.0 / jnp.sqrt(total_sq / entries + epsilon))[0:1, 0:1]

    for a in range(cap):
        wait_for(stage.at[a, pl.ds(0, others)], fsend.at[a])
        wait_for(dirs.at[a, pl.ds(0, others * rows)], rsend.at[a])
    wait_for(sq_group.at[pl.ds(0, others)], qsend.at[0])
    wait_for(sq_all.at[pl.ds(0, mps - 1)], qsend.at[1])
    for a in range(cap):
        wait_for(back.at[a, pl.ds(0, others)], rrecv.at[a])

    def place(j, c):
        s = slot[j]
        update[j] = back[s % cap, s // cap] * scale
        return c

    lax.fori_loop(0, update.shape[0], place, 0, unroll=4)


def finish(update, ls, rs, update_hbm, nl_hbm, nr_hbm, sem):
    pairs = ((update, update_hbm), (ls, nl_hbm), (rs, nr_hbm))
    stores = [pltpu.make_async_copy(a, b, sem.at[i]) for i, (a, b) in enumerate(pairs)]
    for store in stores:
        store.start()
    for store in stores:
        store.wait()


def far(x):
    return pltpu.with_memory_space_constraint(x, pltpu.HBM)


def local(inner, grad, block_slot, left_stat, right_stat, left_root, right_root):
    fs, mps = lax.axis_size("fsdp"), lax.axis_size("mp")
    cap = left_stat.shape[0]
    count, rows, width = grad.shape
    entries = float(count * mps * width * width)
    square = (cap, width, width)
    chunks = (cap, fs, rows, width)
    table = (1, -(-fs * cap // 128) * 128)
    hbm = pl.BlockSpec(memory_space=pltpu.HBM)
    vmem = pl.BlockSpec(memory_space=pltpu.VMEM)
    update, left, right = pl.pallas_call(
        functools.partial(kernel, (fs, mps, cap, rows, width, inner, entries)),
        out_shape=(
            pltpu.VMEM(grad.shape, F32),
            pltpu.VMEM(square, F32),
            pltpu.VMEM(square, F32),
        ),
        in_specs=[hbm] * 6,
        out_specs=(vmem,) * 3,
        scratch_shapes=[
            pltpu.VMEM(chunks, F32),
            pltpu.SMEM(block_slot.shape, jnp.int32),
            pltpu.VMEM(table, jnp.int32),
            pltpu.SMEM(table, jnp.int32),
            pltpu.VMEM(grad.shape, F32),
            pltpu.VMEM(chunks, F32),
            pltpu.VMEM(square, F32),
            pltpu.VMEM(square, F32),
            pltpu.VMEM(square, BF16),
            pltpu.VMEM(square, BF16),
            pltpu.VMEM(square, BF16),
            pltpu.VMEM(square, BF16),
            pltpu.VMEM((1, 128), F32),
            pltpu.VMEM((fs, 1, 128), F32),
            pltpu.VMEM((1, 128), F32),
            pltpu.VMEM((mps, 1, 128), F32),
            pltpu.SemaphoreType.DMA((7,)),
            pltpu.SemaphoreType.DMA((cap,)),
            pltpu.SemaphoreType.DMA((cap,)),
            pltpu.SemaphoreType.DMA((cap,)),
            pltpu.SemaphoreType.DMA((cap,)),
            pltpu.SemaphoreType.DMA((2,)),
            pltpu.SemaphoreType.DMA((2,)),
        ],
        compiler_params=pltpu.CompilerParams(
            collective_id=0, has_side_effects=True, vmem_limit_bytes=40 << 20
        ),
        cost_estimate=pl.CostEstimate(
            flops=20 * cap * width**3, bytes_accessed=12 << 20, transcendentals=0
        ),
    )(
        far(block_slot),
        far(grad),
        far(left_stat[:, 0]),
        far(right_stat[:, 0]),
        far(left_root[:, 0]),
        far(right_root[:, 0]),
    )
    update, new_left, new_right = pl.pallas_call(
        finish,
        out_shape=(
            jax.ShapeDtypeStruct(grad.shape, F32),
            jax.ShapeDtypeStruct(square, F32),
            jax.ShapeDtypeStruct(square, F32),
        ),
        in_specs=[vmem] * 3,
        out_specs=(hbm,) * 3,
        scratch_shapes=[pltpu.SemaphoreType.DMA((3,))],
        compiler_params=pltpu.CompilerParams(vmem_limit_bytes=16 << 20),
        cost_estimate=pl.CostEstimate(flops=0, bytes_accessed=5 << 20, transcendentals=0),
    )(update, left, right)
    return (update, new_left[:, None], new_right[:, None])


def solution(mesh):
    fs = mesh.shape["fsdp"]
    inner = 8 if fs % 8 == 0 else fs
    placed = (
        P("mp", "fsdp", None),
        P("mp"),
        P("fsdp", "mp", None, None),
        P("fsdp", "mp", None, None),
        P("fsdp", "mp", None, None),
        P("fsdp", "mp", None, None),
    )
    return jax.shard_map(
        functools.partial(local, inner),
        mesh=mesh,
        in_specs=placed,
        out_specs=(P("mp", "fsdp", None), P("fsdp", "mp", None, None), P("fsdp", "mp", None, None)),
        check_vma=False,
    )
```

```python
import functools

import jax
import jax.numpy as jnp
from jax import lax
from jax.experimental import pallas as pl
from jax.experimental.pallas import tpu as pltpu
from jax.sharding import PartitionSpec as P

decay_rate = 0.9
epsilon = 1e-06
MESH = pl.DeviceIdType.MESH
F32 = jnp.float32
BF16 = jnp.bfloat16


def split(x):
    high = x.astype(BF16)
    return high, (x - high.astype(F32)).astype(BF16)


def dot(a, b, a_dim=1, b_dim=0):
    return lax.dot_general(a, b, (((a_dim,), (b_dim,)), ((), ())), preferred_element_type=F32)


def kernel(
    cfg,
    slot_hbm,
    grad_hbm,
    ls_hbm,
    rs_hbm,
    lr_hbm,
    rr_hbm,
    update,
    ls,
    rs,
    back,
    slot,
    table,
    source,
    grad,
    stage,
    blocks,
    dirs,
    lr,
    rr,
    high,
    low,
    sq_out,
    sq_group,
    sq_sum,
    sq_all,
    in_sem,
    fsend,
    frecv,
    rsend,
    rrecv,
    qsend,
    qrecv,
):
    fs, mps, cap, rows, width, inner, entries = cfg
    outer = fs // inner
    me = lax.axis_index("fsdp")
    lane = lax.axis_index("mp")
    me_out, me_in = me // inner, me % inner
    tile = 128
    tiles = width // tile

    turn = 1 - 2 * (me_in % 2)

    def zigzag(k, size):
        return (k + 1) // 2 if k % 2 else (size - k // 2) % size

    outs = [((me_out + turn * zigzag(k, outer) + outer) % outer) * inner for k in range(outer)]
    ins = [(me_in + turn * zigzag(k, inner) + inner) % inner for k in range(inner)]
    peers = [outs[d // inner] + ins[d % inner] for d in range(fs)]
    lanes = [(lane + d) % mps for d in range(mps)]

    def peer(d):
        k, j = d // inner, d % inner
        k = (k % 2) * ((k + 1) // 2) + (1 - k % 2) * (outer - k // 2)
        j = (j % 2) * ((j + 1) // 2) + (1 - j % 2) * (inner - j // 2)
        p_out = (me_out + turn * k + outer) % outer
        return p_out * inner + (me_in + turn * j + inner) % inner

    def rows_of(device):
        return pl.ds(pl.multiple_of(device * rows, rows), rows)

    pairs = (
        (slot_hbm, slot),
        (grad_hbm, grad),
        (lr_hbm, lr),
        (rr_hbm, rr),
        (ls_hbm, ls),
        (rs_hbm, rs),
    )
    loads = [pltpu.make_async_copy(a, b, in_sem.at[i]) for i, (a, b) in enumerate(pairs)]
    loads[0].start()
    loads[1].start()

    barrier = pltpu.get_barrier_semaphore()

    for f, l in [(p, lane) for p in peers[1:]] + [(me, l) for l in lanes[1:]]:
        pl.semaphore_signal(barrier, inc=1, device_id=(f, l), device_id_type=MESH)

    loads[0].wait()
    ids = lax.broadcasted_iota(jnp.int32, table.shape, 1)

    def name(j, named):
        return jnp.where(ids == slot[j], j + 1, named)

    table[...] = lax.fori_loop(0, grad.shape[0], name, jnp.zeros(table.shape, jnp.int32))
    move = pltpu.make_async_copy(table, source, in_sem.at[len(pairs)])
    move.start()
    move.wait()
    loads[1].wait()

    for a in range(cap):

        def fill(o, c, a=a):
            named = source[0, o * cap + a]
            chunk = grad[jnp.maximum(named - 1, 0)]
            stage[a, o] = jnp.where(named > 0, chunk, 0.0)
            return c

        lax.fori_loop(0, fs, fill, 0)
        if a == 0:
            pl.semaphore_wait(barrier, fs - 1 + mps - 1)

        def send(d, c, a=a):
            p = peer(d)
            pltpu.make_async_remote_copy(
                src_ref=stage.at[a, p],
                dst_ref=blocks.at[a, rows_of(me)],
                send_sem=fsend.at[a],
                recv_sem=frecv.at[a],
                device_id=(p, lane),
                device_id_type=MESH,
            ).start()
            return c

        lax.fori_loop(1, fs, send, 0)
        blocks[a, rows_of(me)] = stage[a, me]

    for load in loads[2:]:
        load.start()
    for load in loads[2:]:
        load.wait()

    def give_back(a, first, last):
        def send(d, c):
            p = peer(d)
            pltpu.make_async_remote_copy(
                src_ref=dirs.at[a, rows_of(p)],
                dst_ref=back.at[a, me],
                send_sem=rsend.at[a],
                recv_sem=rrecv.at[a],
                device_id=(p, lane),
                device_id_type=MESH,
            ).start()
            return c

        lax.fori_loop(first, last, send, 0)

    def part(t):
        return pl.ds(pl.multiple_of(t * tile, tile), tile)

    def total(x):
        return jnp.sum(x, axis=(0, 1), keepdims=True)

    def precondition(a):
        def cut(t, sq):
            g = blocks[a, part(t)]
            h, l = split(g)
            high[a, part(t)] = h
            low[a, part(t)] = l
            return sq + total(g * g)

        grad_sq = lax.fori_loop(0, tiles, cut, jnp.zeros((1, 1), F32))

        def multiply(t, sq):
            root = lr[a, part(t)]
            h, l = split(dot(root, high[a]) + dot(root, low[a]))
            p = dot(h, rr[a]) + dot(l, rr[a])
            dirs[a, part(t)] = p
            return sq + total(p * p)

        pre_sq = lax.fori_loop(0, tiles, multiply, jnp.zeros((1, 1), F32))
        ratio = jnp.sqrt(grad_sq) / (jnp.sqrt(pre_sq) + epsilon)

        def graft(t, sq):
            p = dirs[a, part(t)] * ratio
            dirs[a, part(t)] = p
            return sq + total(p * p)

        return lax.fori_loop(0, tiles, graft, jnp.zeros((1, 1), F32))

    def statistics(a):
        def left(t, c):
            h, l = high[a, part(t)], low[a, part(t)]
            prod = dot(h, high[a], 1, 1) + dot(h, low[a], 1, 1) + dot(l, high[a], 1, 1)
            ls[a, part(t)] = decay_rate * ls[a, part(t)] + (1.0 - decay_rate) * prod
            return c

        lax.fori_loop(0, tiles, left, 0)
        for t in range(tiles):
            cols = pl.ds(t * tile, tile)
            h, l = high[a, :, cols], low[a, :, cols]
            prod = dot(h, high[a], 0, 0) + dot(h, low[a], 0, 0) + dot(l, high[a], 0, 0)
            rs[a, cols] = decay_rate * rs[a, cols] + (1.0 - decay_rate) * prod

    def wait_for(ref, sem):
        pltpu.make_async_copy(ref, ref, sem).wait()

    others = fs - 1

    def send_square(d, c):
        pltpu.make_async_remote_copy(
            src_ref=sq_out,
            dst_ref=sq_group.at[me],
            send_sem=qsend.at[0],
            recv_sem=qrecv.at[0],
            device_id=(peer(d), lane),
            device_id_type=MESH,
        ).start()
        return c

    def send_sum(d, c):
        pltpu.make_async_remote_copy(
            src_ref=sq_sum,
            dst_ref=sq_all.at[lane],
            send_sem=qsend.at[1],
            recv_sem=qrecv.at[1],
            device_id=(me, (lane + d) % mps),
            device_id_type=MESH,
        ).start()
        return c

    squares = jnp.zeros((1, 1), F32)
    for a in range(cap):
        wait_for(blocks.at[a, pl.ds(0, others * rows)], frecv.at[a])
        squares = squares + precondition(a)
        if a < cap - 1:
            give_back(a, 1, fs)
            statistics(a)
        else:
            give_back(a, 1, fs // 4)
            sq_out[...] = jnp.broadcast_to(squares, sq_out.shape)
            lax.fori_loop(1, fs, send_square, 0)
            sq_group[me] = sq_out[...]
            give_back(a, fs // 4, fs // 2)
            wait_for(sq_group.at[pl.ds(0, others)], qrecv.at[0])
            sq_sum[...] = jnp.sum(sq_group[...], axis=0)
            lax.fori_loop(1, mps, send_sum, 0)
            sq_all[lane] = sq_sum[...]
            give_back(a, fs // 2, fs)
            statistics(a)
        back[a, me] = dirs[a, rows_of(me)]

    wait_for(sq_all.at[pl.ds(0, mps - 1)], qrecv.at[1])
    total_sq = jnp.sum(sq_all[...], axis=0)
    scale = (1.0 / jnp.sqrt(total_sq / entries + epsilon))[0:1, 0:1]

    for a in range(cap):
        wait_for(stage.at[a, pl.ds(0, others)], fsend.at[a])
        wait_for(dirs.at[a, pl.ds(0, others * rows)], rsend.at[a])
    wait_for(sq_group.at[pl.ds(0, others)], qsend.at[0])
    wait_for(sq_all.at[pl.ds(0, mps - 1)], qsend.at[1])
    for a in range(cap):
        wait_for(back.at[a, pl.ds(0, others)], rrecv.at[a])

    def place(j, c):
        s = slot[j]
        update[j] = back[s % cap, s // cap] * scale
        return c

    lax.fori_loop(0, update.shape[0], place, 0, unroll=4)


def finish(update, ls, rs, update_hbm, nl_hbm, nr_hbm, sem):
    pairs = ((update, update_hbm), (ls, nl_hbm), (rs, nr_hbm))
    stores = [pltpu.make_async_copy(a, b, sem.at[i]) for i, (a, b) in enumerate(pairs)]
    for store in stores:
        store.start()
    for store in stores:
        store.wait()


def far(x):
    return pltpu.with_memory_space_constraint(x, pltpu.HBM)


def local(inner, grad, block_slot, left_stat, right_stat, left_root, right_root):
    fs, mps = lax.axis_size("fsdp"), lax.axis_size("mp")
    cap = left_stat.shape[0]
    count, rows, width = grad.shape
    entries = float(count * mps * width * width)
    square = (cap, width, width)
    chunks = (cap, fs, rows, width)
    table = (1, -(-fs * cap // 128) * 128)
    hbm = pl.BlockSpec(memory_space=pltpu.HBM)
    vmem = pl.BlockSpec(memory_space=pltpu.VMEM)
    update, left, right = pl.pallas_call(
        functools.partial(kernel, (fs, mps, cap, rows, width, inner, entries)),
        out_shape=(
            pltpu.VMEM(grad.shape, F32),
            pltpu.VMEM(square, F32),
            pltpu.VMEM(square, F32),
        ),
        in_specs=[hbm] * 6,
        out_specs=(vmem,) * 3,
        scratch_shapes=[
            pltpu.VMEM(chunks, F32),
            pltpu.SMEM(block_slot.shape, jnp.int32),
            pltpu.VMEM(table, jnp.int32),
            pltpu.SMEM(table, jnp.int32),
            pltpu.VMEM(grad.shape, F32),
            pltpu.VMEM(chunks, F32),
            pltpu.VMEM(square, F32),
            pltpu.VMEM(square, F32),
            pltpu.VMEM(square, BF16),
            pltpu.VMEM(square, BF16),
            pltpu.VMEM(square, BF16),
            pltpu.VMEM(square, BF16),
            pltpu.VMEM((1, 128), F32),
            pltpu.VMEM((fs, 1, 128), F32),
            pltpu.VMEM((1, 128), F32),
            pltpu.VMEM((mps, 1, 128), F32),
            pltpu.SemaphoreType.DMA((7,)),
            pltpu.SemaphoreType.DMA((cap,)),
            pltpu.SemaphoreType.DMA((cap,)),
            pltpu.SemaphoreType.DMA((cap,)),
            pltpu.SemaphoreType.DMA((cap,)),
            pltpu.SemaphoreType.DMA((2,)),
            pltpu.SemaphoreType.DMA((2,)),
        ],
        compiler_params=pltpu.CompilerParams(
            collective_id=0, has_side_effects=True, vmem_limit_bytes=40 << 20
        ),
        cost_estimate=pl.CostEstimate(
            flops=20 * cap * width**3, bytes_accessed=12 << 20, transcendentals=0
        ),
    )(
        far(block_slot),
        far(grad),
        far(left_stat[:, 0]),
        far(right_stat[:, 0]),
        far(left_root[:, 0]),
        far(right_root[:, 0]),
    )
    update, new_left, new_right = pl.pallas_call(
        finish,
        out_shape=(
            jax.ShapeDtypeStruct(grad.shape, F32),
            jax.ShapeDtypeStruct(square, F32),
            jax.ShapeDtypeStruct(square, F32),
        ),
        in_specs=[vmem] * 3,
        out_specs=(hbm,) * 3,
        scratch_shapes=[pltpu.SemaphoreType.DMA((3,))],
        compiler_params=pltpu.CompilerParams(vmem_limit_bytes=16 << 20),
        cost_estimate=pl.CostEstimate(flops=0, bytes_accessed=5 << 20, transcendentals=0),
    )(update, left, right)
    return (update, new_left[:, None], new_right[:, None])


def solution(mesh):
    fs = mesh.shape["fsdp"]
    inner = 8 if fs % 8 == 0 else fs
    placed = (
        P("mp", "fsdp", None),
        P("mp"),
        P("fsdp", "mp", None, None),
        P("fsdp", "mp", None, None),
        P("fsdp", "mp", None, None),
        P("fsdp", "mp", None, None),
    )
    return jax.shard_map(
        functools.partial(local, inner),
        mesh=mesh,
        in_specs=placed,
        out_specs=(P("mp", "fsdp", None), P("fsdp", "mp", None, None), P("fsdp", "mp", None, None)),
        check_vma=False,
    )
```
